32 devices in a mesh: row: 4 (over y, core), col: 8 (over z, x).
Axes of the slice: x: 2, y: 2, z: 4, core: 2. Of those that a mesh axis runs over, the one named last changes fastest.
Arguments:
- wavefield: bfloat16 [32768, 2, 128], P(('col', 'row')), may hold values from -6 to 6
- recorded: bfloat16 [32768, 2, 128], P(('row', 'col')), may hold values from -6 to 6
- v_bases: bfloat16 [128, 128, 32, 256], P('row', 'col'), may hold values from -0.25 to 0.25
- u_bases: bfloat16 [128, 128, 32, 256], P(('row', 'col')), may hold values from -0.09375 to 0.09375
- ranks: int32 [128, 128], P('row', 'col'), may hold values from 1 to 16
Outputs:
- residual: float32 [32768, 2, 128], P(('row', 'col'))
- gradient: float32 [32768, 2, 128], P(('col', 'row'))
The draws below stay inside these ranges and needn't reach their ends.
Inputs may be any that keep to these rules, and one draw needn't show every extreme that they name: `ranks`: some tile has rank 16.
All inputs are finite; a program needn't handle non-finite values.
Results may differ from the reference program's by a relative error of at most 0.0038.
Values may be sent and summed in bfloat16 or wider, within the bound.
A program may use at most 128 MiB of HBM per device.

```python
import jax
import jax.numpy as jnp
from jax import lax

TILE = 256
RK = 16
S = 128
NTR = 128
NTC = 128
NREC = 32768
NSRC = 32768


def set_ends(result, rng, smallest, high):
    shape = result.shape
    spot = [jax.random.randint(jax.random.fold_in(rng, axis), (), 0, shape[axis]) for axis in range(len(shape))]
    result = result.at[tuple(spot)].set(smallest)
    longest = shape.index(max(shape))
    spot[longest] = (spot[longest] + 1) % shape[longest]
    return result.at[tuple(spot)].set(high)


def block_scale(key, shape, pieces, least, top_value):
    factor_of = 1.0
    for dim, shards_of in pieces:
        heights = jax.random.uniform(jax.random.fold_in(jax.random.fold_in(key, 6), dim), (shards_of,), jnp.float32, least / len(pieces), top_value / len(pieces))
        factor_of = factor_of * jnp.repeat(jnp.exp(heights), shape[dim] // shards_of).reshape((-1,) + (1,) * (len(shape) - 1 - dim))
    return factor_of


def noise(own_key, dims, scale, bound, split=(), held_as=jnp.bfloat16):
    array = scale * jax.random.normal(own_key, dims, jnp.float32)
    if split:
        array = array * block_scale(own_key, dims, split, -0.22, 0.18)
    return jnp.clip(array, -bound, bound).astype(held_as)


def setup_inputs(seed: int = 0) -> dict:
    key_list = jax.random.split(jax.random.key(seed), 6)
    wavefield = noise(key_list[0], (NSRC, 2, S), 1.0, 6.0, ((0, 32),))
    recorded = noise(key_list[1], (NREC, 2, S), 1.0, 6.0, ((0, 32),))
    v_bases = noise(key_list[2], (NTR, NTC, 2 * RK, TILE), (2 * TILE) ** -0.5, 0.25, ((0, 4), (1, 8)))
    u_bases = noise(key_list[3], (NTR, NTC, 2 * RK, TILE), (2 * RK * NTC) ** -0.5, 0.09375, ((0, 32),))
    ranks = set_ends(jax.random.randint(key_list[4], (NTR, NTC), 1, RK + 1), jax.random.fold_in(key_list[4], 1), 1, RK).astype(jnp.int32)
    return dict(wavefield=wavefield, recorded=recorded, v_bases=v_bases, u_bases=u_bases, ranks=ranks)


def combine_adjoint(prod):
    half = prod.shape[2] // 2
    real = prod[:, :, :half, 0] + prod[:, :, half:, 1]
    imag = prod[:, :, :half, 1] - prod[:, :, half:, 0]
    return jnp.stack([real, imag], axis=3)


def stacked(coeffs):
    real = coeffs[:, :, :, 0]
    imag = coeffs[:, :, :, 1]
    first = jnp.concatenate([real, -imag], axis=2)
    second = jnp.concatenate([imag, real], axis=2)
    return jnp.stack([first, second], axis=3)


def reference(wavefield, recorded, v_bases, u_bases, ranks):
    blocks = wavefield.astype(jnp.float32).reshape(NTC, TILE, 2, S)
    levels = lax.broadcasted_iota(jnp.int32, (NTR, NTC, RK), 2)
    mask = (levels < ranks[:, :, None]).astype(jnp.float32)
    rows = recorded.reshape(NTR, TILE, 2, S)

    def step(total, item):
        v_row, u_row, m_row, d_row = item
        v_row = v_row[None].astype(jnp.float32)
        u_row = u_row[None].astype(jnp.float32)
        m_row = m_row[None]
        prod = jnp.einsum("ijrk,jkcs->ijrcs", v_row, blocks)
        coeffs = (combine_adjoint(prod) * m_row[:, :, :, None, None]).astype(jnp.bfloat16)
        modelled = jnp.einsum("ijrk,ijrcs->ikcs", u_row, stacked(coeffs.astype(jnp.float32)))[0]
        res_row = modelled - d_row.astype(jnp.float32)
        rounded = res_row.astype(jnp.bfloat16).astype(jnp.float32)
        prod_back = jnp.einsum("ijrk,ikcs->ijrcs", u_row, rounded[None])
        back = combine_adjoint(prod_back).astype(jnp.bfloat16).astype(jnp.float32)
        back = back * m_row[:, :, :, None, None]
        total = total + jnp.einsum("ijrk,ijrcs->jkcs", v_row, stacked(back))
        return total, res_row

    start = jnp.zeros((NTC, TILE, 2, S), jnp.float32)
    total, res_rows = lax.scan(step, start, (v_bases, u_bases, mask, rows))
    return res_rows.reshape(NREC, 2, S), total.reshape(NSRC, 2, S)
```

```python
import functools

import jax
import jax.numpy as jnp
from jax import lax
from jax.experimental import pallas as pl
from jax.experimental.pallas import tpu as pltpu
from jax.sharding import PartitionSpec as P

MESH = pl.DeviceIdType.MESH


def adjoint_pair(prod, half):
    sources = prod.shape[-1] // 2
    prod = prod.reshape(-1, 2, half, 2 * sources)
    first, second = prod[:, 0], prod[:, 1]
    real = first[..., :sources] + second[..., sources:]
    imag = first[..., sources:] - second[..., :sources]
    return jnp.concatenate([real, imag], axis=-1)


def stacked(coeffs):
    sources = coeffs.shape[-1] // 2
    real, imag = coeffs[..., :sources], coeffs[..., sources:]
    second = jnp.concatenate([-imag, real], axis=-1)
    both = jnp.concatenate([coeffs, second], axis=1)
    return both.reshape(-1, 2 * sources)


def flat(bases):
    return bases.reshape(-1, bases.shape[-1])


def transposed_dot(left, right):
    return lax.dot_general(left, right, (((0,), (0,)), ((), ())), preferred_element_type=jnp.float32)


def kernel(
    n_row, n_col, wave, rec, v, u, ranks, res, grad,
    x, send1, recv1, send2, recv2, total, rs1, sb, rs2,
    xs, xr, s1, r1, s2, r2, gs1, gr1, gs2, gr2,
):
    row, col = lax.axis_index("row"), lax.axis_index("col")
    y, core = row // 2, row % 2
    n_y = n_row // 2
    tiles, columns = u.shape[0], v.shape[2]
    half = v.shape[3] // 2
    width = wave.shape[0]
    level = lax.broadcasted_iota(jnp.int32, (half, x.shape[2]), 0)

    barrier = pltpu.get_barrier_semaphore()
    for k in range(1, n_col):
        pl.semaphore_signal(barrier, inc=1, device_id={"col": lax.rem(col + k, n_col)}, device_id_type=MESH)
    for k in range(1, n_row):
        pl.semaphore_signal(barrier, inc=1, device_id={"row": lax.rem(row + k, n_row)}, device_id_type=MESH)
    pl.semaphore_wait(barrier, n_col + n_row - 2)

    def wave_copy(peer, origin):
        return pltpu.make_async_remote_copy(
            src_ref=wave, dst_ref=x.at[pl.ds(origin * width, width)],
            send_sem=xs.at[peer], recv_sem=xr.at[origin],
            device_id={"row": peer}, device_id_type=MESH)

    def exchange(src, dst, send_sem, recv_sem, a, peer, origin):
        return pltpu.make_async_remote_copy(
            src_ref=src.at[a, peer], dst_ref=dst.at[a, origin],
            send_sem=send_sem.at[a, peer], recv_sem=recv_sem.at[a, origin],
            device_id={"col": peer}, device_id_type=MESH)

    for k in range(1, n_row):
        wave_copy(lax.rem(row + k, n_row), row).start()
    x[pl.ds(row * width, width)] = wave[...]
    total[...] = jnp.zeros_like(total)
    for a in range(tiles):
        res[a] = -rec[a].astype(jnp.float32)
    for k in range(1, n_row):
        peer = lax.rem(row + k, n_row)
        wave_copy(peer, peer).wait_recv()

    def forward(a, carry):
        def one(j, carry):
            prod = jnp.dot(flat(v[:, a, j]), x[j], preferred_element_type=jnp.float32)
            coeffs = adjoint_pair(prod, half)
            for d in range(n_col):
                kept = jnp.where(level < ranks[d * tiles + a, j], coeffs[d], 0.0)
                send1[a, d, j] = kept.astype(jnp.bfloat16)
            return carry

        lax.fori_loop(0, columns, one, 0)
        for k in range(1, n_col):
            exchange(send1, recv1, s1, r1, a, lax.rem(col + k, n_col), col).start()
        recv1[a, col] = send1[a, col]
        return carry

    lax.fori_loop(0, tiles, forward, 0)

    def middle(a, carry):
        def apply(k, carry):
            origin = lax.rem(col + n_col - k, n_col)

            @pl.when(k > 0)
            def _():
                exchange(send1, recv1, s1, r1, a, origin, origin).wait_recv()

            res[a] += transposed_dot(flat(u[a, origin]), stacked(recv1[a, origin]))
            return carry

        lax.fori_loop(0, n_col, apply, 0)
        rounded = res[a].astype(jnp.bfloat16)

        def project(k, carry):
            peer = lax.rem(col + k, n_col)
            prod = jnp.dot(flat(u[a, peer]), rounded, preferred_element_type=jnp.float32)
            send2[a, peer] = adjoint_pair(prod, half).astype(jnp.bfloat16)

            @pl.when(k < n_col)
            def _():
                exchange(send2, recv2, s2, r2, a, peer, col).start()

            return carry

        lax.fori_loop(1, n_col + 1, project, 0)
        recv2[a, col] = send2[a, col]
        return carry

    lax.fori_loop(0, tiles, middle, 0)

    def last(a, carry):
        for k in range(1, n_col):
            origin = lax.rem(col + n_col - k, n_col)
            exchange(send2, recv2, s2, r2, a, origin, origin).wait_recv()

        def one(j, carry):
            kept = [
                jnp.where(level < ranks[s * tiles + a, j], recv2[a, s, j].astype(jnp.float32), 0.0).astype(jnp.bfloat16)
                for s in range(n_col)
            ]
            total[j] += transposed_dot(flat(v[:, a, j]), stacked(jnp.stack(kept)))
            return carry

        lax.fori_loop(0, columns, one, 0)
        return carry

    lax.fori_loop(0, tiles, last, 0)

    def core_copy(k):
        return pltpu.make_async_remote_copy(
            src_ref=total.at[pl.ds((2 * k + 1 - core) * width, width)], dst_ref=rs1.at[k],
            send_sem=gs1.at[k], recv_sem=gr1.at[k],
            device_id={"row": 2 * y + 1 - core}, device_id_type=MESH)

    def chip_copy(peer, origin):
        return pltpu.make_async_remote_copy(
            src_ref=sb.at[peer], dst_ref=rs2.at[origin],
            send_sem=gs2.at[peer], recv_sem=gr2.at[origin],
            device_id={"row": 2 * peer + core}, device_id_type=MESH)

    order = [lax.rem(y + k, n_y) for k in range(1, n_y)]
    for peer in order + [y]:
        core_copy(peer).start()
    for peer in order:
        core_copy(peer).wait_recv()
        here = total[pl.ds((2 * peer + core) * width, width)]
        sb[peer] = (here + rs1[peer]).astype(jnp.bfloat16)
        chip_copy(peer, y).start()
    core_copy(y).wait_recv()
    grad[...] = total[pl.ds(row * width, width)] + rs1[y]
    for peer in order:
        chip_copy(peer, peer).wait_recv()
        grad[...] += rs2[peer].astype(jnp.float32)

    for k in range(1, n_row):
        wave_copy(lax.rem(row + k, n_row), row).wait_send()
    for k in range(n_y):
        core_copy(k).wait_send()
    for peer in order:
        chip_copy(peer, y).wait_send()

    def drain(a, carry):
        for k in range(1, n_col):
            peer = lax.rem(col + k, n_col)
            exchange(send1, recv1, s1, r1, a, peer, col).wait_send()
            exchange(send2, recv2, s2, r2, a, peer, col).wait_send()
        return carry

    lax.fori_loop(0, tiles, drain, 0)


def body(n_row, n_col, wavefield, recorded, v_bases, u_bases, ranks):
    tile, sources = v_bases.shape[3], wavefield.shape[2]
    both, half = v_bases.shape[2], v_bases.shape[2] // 2
    tiles, columns = u_bases.shape[0], v_bases.shape[1]
    wide = 2 * sources
    width = columns // n_row
    vmem = pl.BlockSpec(memory_space=pltpu.VMEM)
    trade = pltpu.VMEM((tiles, n_col, columns, half, wide), jnp.bfloat16)
    dma = pltpu.SemaphoreType.DMA
    residual, gradient = pl.pallas_call(
        functools.partial(kernel, n_row, n_col),
        out_shape=(
            jax.ShapeDtypeStruct((tiles, tile, wide), jnp.float32),
            jax.ShapeDtypeStruct((width, tile, wide), jnp.float32),
        ),
        in_specs=[vmem, vmem, vmem, vmem, pl.BlockSpec(memory_space=pltpu.SMEM)],
        out_specs=(vmem, vmem),
        scratch_shapes=[
            pltpu.VMEM((columns, tile, wide), jnp.bfloat16),
            trade, trade, trade, trade,
            pltpu.VMEM((columns, tile, wide), jnp.float32),
            pltpu.VMEM((n_row // 2, width, tile, wide), jnp.float32),
            pltpu.VMEM((n_row // 2, width, tile, wide), jnp.bfloat16),
            pltpu.VMEM((n_row // 2, width, tile, wide), jnp.bfloat16),
            dma((n_row,)), dma((n_row,)),
            dma((tiles, n_col)), dma((tiles, n_col)), dma((tiles, n_col)), dma((tiles, n_col)),
            dma((n_row // 2,)), dma((n_row // 2,)), dma((n_row // 2,)), dma((n_row // 2,)),
        ],
        compiler_params=pltpu.CompilerParams(
            collective_id=0, has_side_effects=True, vmem_limit_bytes=58 * 2**20
        ),
    )(
        wavefield.reshape(width, tile, wide),
        recorded.reshape(tiles, tile, wide),
        v_bases.reshape(n_col, tiles, columns, both, tile),
        u_bases.reshape(tiles, n_col, columns, both, tile),
        ranks,
    )
    return residual.reshape(-1, 2, sources), gradient.reshape(-1, 2, sources)


def solution(mesh):
    in_specs = (
        P(("col", "row"), None, None),
        P(("row", "col"), None, None),
        P("row", "col", None, None),
        P(("row", "col"), None, None, None),
        P("row", "col"),
    )
    out_specs = (P(("row", "col"), None, None), P(("col", "row"), None, None))
    part = functools.partial(body, mesh.shape["row"], mesh.shape["col"])
    return jax.shard_map(part, mesh=mesh, in_specs=in_specs, out_specs=out_specs, check_vma=False)
```

```python
import functools

import jax
import jax.numpy as jnp
from jax import lax
from jax.experimental import pallas as pl
from jax.experimental.pallas import tpu as pltpu
from jax.sharding import PartitionSpec as P

MESH = pl.DeviceIdType.MESH


def adjoint_pair(prod, half):
    sources = prod.shape[-1] // 2
    prod = prod.reshape(-1, 2, half, 2 * sources)
    first, second = prod[:, 0], prod[:, 1]
    real = first[..., :sources] + second[..., sources:]
    imag = first[..., sources:] - second[..., :sources]
    return jnp.concatenate([real, imag], axis=-1)


def stacked(coeffs):
    sources = coeffs.shape[-1] // 2
    real, imag = coeffs[..., :sources], coeffs[..., sources:]
    second = jnp.concatenate([-imag, real], axis=-1)
    both = jnp.concatenate([coeffs, second], axis=1)
    return both.reshape(-1, 2 * sources)


def flat(bases):
    return bases.reshape(-1, bases.shape[-1])


def transposed_dot(left, right):
    return lax.dot_general(left, right, (((0,), (0,)), ((), ())), preferred_element_type=jnp.float32)


def kernel(
    n_row, n_col, wave, rec, v_hbm, u_hbm, ranks, res, grad,
    v, u, x, send1, recv1, send2, recv2, total, rs1, sb, rs2,
    vs, us, xs, xr, s1, r1, s2, r2, gs1, gr1, gs2, gr2,
):
    row, col = lax.axis_index("row"), lax.axis_index("col")
    y, core = row // 2, row % 2
    n_y = n_row // 2
    tiles, columns = u.shape[0], v.shape[2]
    half = v.shape[3] // 2
    width = wave.shape[0]
    group = 2 * width
    level = lax.broadcasted_iota(jnp.int32, (half, x.shape[2]), 0)

    def v_copy(part):
        span = pl.ds(part * group, group)
        return pltpu.make_async_copy(v_hbm.at[:, :, span], v.at[:, :, span], vs.at[part])

    u_copy = pltpu.make_async_copy(u_hbm, u, us)
    for k in range(n_y):
        v_copy(lax.rem(y + k, n_y)).start()
    u_copy.start()

    barrier = pltpu.get_barrier_semaphore()
    for k in range(1, n_col):
        pl.semaphore_signal(barrier, inc=1, device_id={"col": lax.rem(col + k, n_col)}, device_id_type=MESH)
    for k in range(1, n_row):
        pl.semaphore_signal(barrier, inc=1, device_id={"row": lax.rem(row + k, n_row)}, device_id_type=MESH)
    pl.semaphore_wait(barrier, n_col + n_row - 2)

    def wave_copy(peer, origin):
        return pltpu.make_async_remote_copy(
            src_ref=wave, dst_ref=x.at[pl.ds(origin * width, width)],
            send_sem=xs.at[peer], recv_sem=xr.at[origin],
            device_id={"row": peer}, device_id_type=MESH)

    def exchange(src, dst, send_sem, recv_sem, a, peer, origin, part):
        span = pl.ds(part * group, group)
        return pltpu.make_async_remote_copy(
            src_ref=src.at[a, peer, span], dst_ref=dst.at[a, origin, span],
            send_sem=send_sem.at[a, peer, part], recv_sem=recv_sem.at[a, origin, part],
            device_id={"col": peer}, device_id_type=MESH)

    wave_copy(2 * y + 1 - core, row).start()
    for k in range(1, n_y):
        for c in range(2):
            wave_copy(2 * lax.rem(y + k, n_y) + c, row).start()
    x[pl.ds(row * width, width)] = wave[...]
    total[...] = jnp.zeros_like(total)
    for a in range(tiles):
        res[a] = -rec[a].astype(jnp.float32)

    for step in range(n_y):
        part = lax.rem(y + step, n_y)
        if step == 0:
            sibling = 2 * y + 1 - core
            wave_copy(sibling, sibling).wait_recv()
        else:
            for c in range(2):
                wave_copy(2 * part + c, 2 * part + c).wait_recv()
        v_copy(part).wait()

        def forward(a, carry):
            def one(t, carry):
                j = part * group + t
                prod = jnp.dot(flat(v[:, a, j]), x[j], preferred_element_type=jnp.float32)
                coeffs = adjoint_pair(prod, half)
                for d in range(n_col):
                    kept = jnp.where(level < ranks[d * tiles + a, j], coeffs[d], 0.0)
                    send1[a, d, j] = kept.astype(jnp.bfloat16)
                return carry

            lax.fori_loop(0, group, one, 0)
            for k in range(1, n_col):
                exchange(send1, recv1, s1, r1, a, lax.rem(col + k, n_col), col, part).start()
            span = pl.ds(part * group, group)
            recv1[a, col, span] = send1[a, col, span]
            return carry

        lax.fori_loop(0, tiles, forward, 0)

    u_copy.wait()

    def middle(a, carry):
        def apply(k, carry):
            origin = lax.rem(col + n_col - k, n_col)

            @pl.when(k > 0)
            def _():
                for part in range(n_y):
                    exchange(send1, recv1, s1, r1, a, origin, origin, part).wait_recv()

            res[a] += transposed_dot(flat(u[a, origin]), stacked(recv1[a, origin]))
            return carry

        lax.fori_loop(0, n_col, apply, 0)
        rounded = res[a].astype(jnp.bfloat16)

        def project(k, carry):
            peer = lax.rem(col + k, n_col)
            prod = jnp.dot(flat(u[a, peer]), rounded, preferred_element_type=jnp.float32)
            send2[a, peer] = adjoint_pair(prod, half).astype(jnp.bfloat16)

            @pl.when(k < n_col)
            def _():
                for step in range(1, n_y):
                    exchange(send2, recv2, s2, r2, a, peer, col, lax.rem(y + step, n_y)).start()

            return carry

        lax.fori_loop(1, n_col + 1, project, 0)
        for k in range(1, n_col):
            exchange(send2, recv2, s2, r2, a, lax.rem(col + k, n_col), col, y).start()
        recv2[a, col] = send2[a, col]
        return carry

    lax.fori_loop(0, tiles, middle, 0)

    def last(a, part):
        for k in range(1, n_col):
            origin = lax.rem(col + n_col - k, n_col)
            exchange(send2, recv2, s2, r2, a, origin, origin, part).wait_recv()

        def one(t, carry):
            j = part * group + t
            kept = [
                jnp.where(level < ranks[s * tiles + a, j], recv2[a, s, j].astype(jnp.float32), 0.0).astype(jnp.bfloat16)
                for s in range(n_col)
            ]
            total[j] += transposed_dot(flat(v[:, a, j]), stacked(jnp.stack(kept)))
            return carry

        lax.fori_loop(0, group, one, 0)

    def early(a, carry):
        for step in range(1, n_y + 1):
            last(a, lax.rem(y + step, n_y))
        return carry

    lax.fori_loop(0, tiles - 1, early, 0)

    def core_copy(k):
        return pltpu.make_async_remote_copy(
            src_ref=total.at[pl.ds((2 * k + 1 - core) * width, width)], dst_ref=rs1.at[k],
            send_sem=gs1.at[k], recv_sem=gr1.at[k],
            device_id={"row": 2 * y + 1 - core}, device_id_type=MESH)

    def chip_copy(peer, origin):
        return pltpu.make_async_remote_copy(
            src_ref=sb.at[peer], dst_ref=rs2.at[origin],
            send_sem=gs2.at[peer], recv_sem=gr2.at[origin],
            device_id={"row": 2 * peer + core}, device_id_type=MESH)

    order = [lax.rem(y + k, n_y) for k in range(1, n_y)]
    for peer in order:
        last(tiles - 1, peer)
        core_copy(peer).start()
    for peer in order:
        core_copy(peer).wait_recv()
        here = total[pl.ds((2 * peer + core) * width, width)]
        sb[peer] = (here + rs1[peer]).astype(jnp.bfloat16)
        chip_copy(peer, y).start()
    last(tiles - 1, y)
    core_copy(y).start()
    core_copy(y).wait_recv()
    grad[...] = total[pl.ds(row * width, width)] + rs1[y]
    for peer in order:
        chip_copy(peer, peer).wait_recv()
        grad[...] += rs2[peer].astype(jnp.float32)

    for k in range(1, n_row):
        wave_copy(lax.rem(row + k, n_row), row).wait_send()
    for k in range(n_y):
        core_copy(k).wait_send()
    for peer in order:
        chip_copy(peer, y).wait_send()

    def drain(a, carry):
        for k in range(1, n_col):
            peer = lax.rem(col + k, n_col)
            for part in range(n_y):
                exchange(send1, recv1, s1, r1, a, peer, col, part).wait_send()
                exchange(send2, recv2, s2, r2, a, peer, col, part).wait_send()
        return carry

    lax.fori_loop(0, tiles, drain, 0)


def body(n_row, n_col, wavefield, recorded, v_bases, u_bases, ranks):
    tile, sources = v_bases.shape[3], wavefield.shape[2]
    both, half = v_bases.shape[2], v_bases.shape[2] // 2
    tiles, columns = u_bases.shape[0], v_bases.shape[1]
    wide = 2 * sources
    width = columns // n_row
    vmem = pl.BlockSpec(memory_space=pltpu.VMEM)
    whole = pl.BlockSpec(memory_space=pl.ANY)
    n_y = n_row // 2
    trade = pltpu.VMEM((tiles, n_col, columns, half, wide), jnp.bfloat16)
    dma = pltpu.SemaphoreType.DMA
    pair = dma((tiles, n_col, n_y))
    residual, gradient = pl.pallas_call(
        functools.partial(kernel, n_row, n_col),
        out_shape=(
            jax.ShapeDtypeStruct((tiles, tile, wide), jnp.float32),
            jax.ShapeDtypeStruct((width, tile, wide), jnp.float32),
        ),
        in_specs=[vmem, vmem, whole, whole, pl.BlockSpec(memory_space=pltpu.SMEM)],
        out_specs=(vmem, vmem),
        scratch_shapes=[
            pltpu.VMEM((n_col, tiles, columns, both, tile), jnp.bfloat16),
            pltpu.VMEM((tiles, n_col, columns, both, tile), jnp.bfloat16),
            pltpu.VMEM((columns, tile, wide), jnp.bfloat16),
            trade, trade, trade, trade,
            pltpu.VMEM((columns, tile, wide), jnp.float32),
            pltpu.VMEM((n_row // 2, width, tile, wide), jnp.float32),
            pltpu.VMEM((n_row // 2, width, tile, wide), jnp.bfloat16),
            pltpu.VMEM((n_row // 2, width, tile, wide), jnp.bfloat16),
            dma((n_y,)), dma, dma((n_row,)), dma((n_row,)),
            pair, pair, pair, pair,
            dma((n_row // 2,)), dma((n_row // 2,)), dma((n_row // 2,)), dma((n_row // 2,)),
        ],
        compiler_params=pltpu.CompilerParams(
            collective_id=0, has_side_effects=True, vmem_limit_bytes=58 * 2**20
        ),
    )(
        wavefield.reshape(width, tile, wide),
        recorded.reshape(tiles, tile, wide),
        v_bases.reshape(n_col, tiles, columns, both, tile),
        u_bases.reshape(tiles, n_col, columns, both, tile),
        ranks,
    )
    return residual.reshape(-1, 2, sources), gradient.reshape(-1, 2, sources)


def solution(mesh):
    in_specs = (
        P(("col", "row"), None, None),
        P(("row", "col"), None, None),
        P("row", "col", None, None),
        P(("row", "col"), None, None, None),
        P("row", "col"),
    )
    out_specs = (P(("row", "col"), None, None), P(("col", "row"), None, None))
    part = functools.partial(body, mesh.shape["row"], mesh.shape["col"])
    return jax.shard_map(part, mesh=mesh, in_specs=in_specs, out_specs=out_specs, check_vma=False)
```

```python
import functools

import jax
import jax.numpy as jnp
from jax import lax
from jax.experimental import pallas as pl
from jax.experimental.pallas import tpu as pltpu
from jax.sharding import PartitionSpec as P

MESH = pl.DeviceIdType.MESH


def adjoint_pair(prod, half):
    sources = prod.shape[-1] // 2
    prod = prod.reshape(-1, 2, half, 2 * sources)
    first, second = prod[:, 0], prod[:, 1]
    real = first[..., :sources] + second[..., sources:]
    imag = first[..., sources:] - second[..., :sources]
    return jnp.concatenate([real, imag], axis=-1)


def stacked(coeffs):
    sources = coeffs.shape[-1] // 2
    real, imag = coeffs[..., :sources], coeffs[..., sources:]
    second = jnp.concatenate([-imag, real], axis=-1)
    both = jnp.concatenate([coeffs, second], axis=1)
    return both.reshape(-1, 2 * sources)


def flat(bases):
    return bases.reshape(-1, bases.shape[-1])


def transposed_dot(left, right):
    return lax.dot_general(left, right, (((0,), (0,)), ((), ())), preferred_element_type=jnp.float32)


def kernel(
    n_row, n_col, wave, rec, v_hbm, u_hbm, ranks, res_out, grad_out,
    res, v, u, x, send1, recv1, send2, recv2, total, rs1, sb, rs2,
    vs, us, xs, xr, s1, r1, s2, r2, gs1, gr1, gs2, gr2,
):
    row, col = lax.axis_index("row"), lax.axis_index("col")
    y, core = row // 2, row % 2
    n_y = n_row // 2
    tiles, columns = u.shape[0], v.shape[2]
    half = v.shape[3] // 2
    width = wave.shape[0]
    group = 2 * width
    level = lax.broadcasted_iota(jnp.int32, (half, x.shape[2]), 0)

    def v_copy(part):
        span = pl.ds(part * group, group)
        return pltpu.make_async_copy(v_hbm.at[:, :, span], v.at[:, :, span], vs.at[part])

    u_copy = pltpu.make_async_copy(u_hbm, u, us)
    for k in range(n_y):
        v_copy(lax.rem(y + k, n_y)).start()
    u_copy.start()

    barrier = pltpu.get_barrier_semaphore()
    for k in range(1, n_col):
        pl.semaphore_signal(barrier, inc=1, device_id={"col": lax.rem(col + k, n_col)}, device_id_type=MESH)
    for k in range(1, n_row):
        pl.semaphore_signal(barrier, inc=1, device_id={"row": lax.rem(row + k, n_row)}, device_id_type=MESH)
    pl.semaphore_wait(barrier, n_col + n_row - 2)

    def wave_copy(peer, origin):
        return pltpu.make_async_remote_copy(
            src_ref=wave, dst_ref=x.at[pl.ds(origin * width, width)],
            send_sem=xs.at[peer], recv_sem=xr.at[origin],
            device_id={"row": peer}, device_id_type=MESH)

    def exchange(src, dst, send_sem, recv_sem, a, peer, origin, part):
        span = pl.ds(part * group, group)
        return pltpu.make_async_remote_copy(
            src_ref=src.at[a, peer, span], dst_ref=dst.at[a, origin, span],
            send_sem=send_sem.at[a, peer, part], recv_sem=recv_sem.at[a, origin, part],
            device_id={"col": peer}, device_id_type=MESH)

    wave_copy(2 * y + 1 - core, row).start()
    for k in range(1, n_y):
        for c in range(2):
            wave_copy(2 * lax.rem(y + k, n_y) + c, row).start()
    x[pl.ds(row * width, width)] = wave[...]
    total[...] = jnp.zeros_like(total)
    for step in range(n_y):
        part = lax.rem(y + step, n_y)
        if step == 0:
            sibling = 2 * y + 1 - core
            wave_copy(sibling, sibling).wait_recv()
        else:
            for c in range(2):
                wave_copy(2 * part + c, 2 * part + c).wait_recv()
        v_copy(part).wait()

        def forward(a, carry):
            def one(t, carry):
                j = part * group + t
                prod = jnp.dot(flat(v[:, a, j]), x[j], preferred_element_type=jnp.float32)
                coeffs = adjoint_pair(prod, half)
                for d in range(n_col):
                    kept = jnp.where(level < ranks[j, d * tiles + a], coeffs[d], 0.0)
                    send1[a, d, j] = kept.astype(jnp.bfloat16)
                return carry

            lax.fori_loop(0, group, one, 0)
            for k in range(1, n_col):
                exchange(send1, recv1, s1, r1, a, lax.rem(col + k, n_col), col, part).start()
            span = pl.ds(part * group, group)
            recv1[a, col, span] = send1[a, col, span]
            return carry

        lax.fori_loop(0, tiles, forward, 0)

    u_copy.wait()
    tile, sources = x.shape[1], x.shape[2] // 2
    for a in range(tiles):
        rows = rec[pl.ds(a * tile, tile)].astype(jnp.float32)
        res[a] = -jnp.concatenate([rows[:, 0], rows[:, 1]], axis=-1)

    def middle(a, carry):
        def apply(k, carry):
            origin = lax.rem(col + n_col - k, n_col)

            @pl.when(k > 0)
            def _():
                for part in range(n_y):
                    exchange(send1, recv1, s1, r1, a, origin, origin, part).wait_recv()

            res[a] += transposed_dot(flat(u[a, origin]), stacked(recv1[a, origin]))
            return carry

        lax.fori_loop(0, n_col, apply, 0)
        rounded = res[a].astype(jnp.bfloat16)

        def project(k, carry):
            peer = lax.rem(col + k, n_col)
            prod = jnp.dot(flat(u[a, peer]), rounded, preferred_element_type=jnp.float32)
            send2[a, peer] = adjoint_pair(prod, half).astype(jnp.bfloat16)

            @pl.when(k < n_col)
            def _():
                for step in range(1, n_y):
                    exchange(send2, recv2, s2, r2, a, peer, col, lax.rem(y + step, n_y)).start()

            return carry

        lax.fori_loop(1, n_col + 1, project, 0)
        for k in range(1, n_col):
            exchange(send2, recv2, s2, r2, a, lax.rem(col + k, n_col), col, y).start()
        recv2[a, col] = send2[a, col]
        for c in range(2):
            res_out[pl.ds(a * tile, tile), c] = res[a, :, c * sources:(c + 1) * sources]
        return carry

    lax.fori_loop(0, tiles, middle, 0)

    def last(a, part):
        for k in range(1, n_col):
            origin = lax.rem(col + n_col - k, n_col)
            exchange(send2, recv2, s2, r2, a, origin, origin, part).wait_recv()

        def one(t, carry):
            j = part * group + t
            kept = [
                jnp.where(level < ranks[j, s * tiles + a], recv2[a, s, j].astype(jnp.float32), 0.0).astype(jnp.bfloat16)
                for s in range(n_col)
            ]
            total[j] += transposed_dot(flat(v[:, a, j]), stacked(jnp.stack(kept)))
            return carry

        lax.fori_loop(0, group, one, 0)

    def early(a, carry):
        for step in range(1, n_y + 1):
            last(a, lax.rem(y + step, n_y))
        return carry

    lax.fori_loop(0, tiles - 1, early, 0)

    def core_copy(k):
        return pltpu.make_async_remote_copy(
            src_ref=total.at[pl.ds((2 * k + 1 - core) * width, width)], dst_ref=rs1.at[k],
            send_sem=gs1.at[k], recv_sem=gr1.at[k],
            device_id={"row": 2 * y + 1 - core}, device_id_type=MESH)

    def chip_copy(peer, origin):
        return pltpu.make_async_remote_copy(
            src_ref=sb.at[peer], dst_ref=rs2.at[origin],
            send_sem=gs2.at[peer], recv_sem=gr2.at[origin],
            device_id={"row": 2 * peer + core}, device_id_type=MESH)

    order = [lax.rem(y + k, n_y) for k in range(1, n_y)]
    for peer in order:
        last(tiles - 1, peer)
        core_copy(peer).start()
    for peer in order:
        core_copy(peer).wait_recv()
        here = total[pl.ds((2 * peer + core) * width, width)]
        sb[peer] = (here + rs1[peer]).astype(jnp.bfloat16)
        chip_copy(peer, y).start()
    last(tiles - 1, y)
    core_copy(y).start()
    core_copy(y).wait_recv()
    for peer in order:
        chip_copy(peer, peer).wait_recv()
    for t in range(width):
        grad = total[row * width + t] + rs1[y, t]
        for peer in order:
            grad += rs2[peer, t].astype(jnp.float32)
        for c in range(2):
            grad_out[pl.ds(t * tile, tile), c] = grad[:, c * sources:(c + 1) * sources]

    for k in range(1, n_row):
        wave_copy(lax.rem(row + k, n_row), row).wait_send()
    for k in range(n_y):
        core_copy(k).wait_send()
    for peer in order:
        chip_copy(peer, y).wait_send()

    def drain(a, carry):
        for k in range(1, n_col):
            peer = lax.rem(col + k, n_col)
            for part in range(n_y):
                exchange(send1, recv1, s1, r1, a, peer, col, part).wait_send()
                exchange(send2, recv2, s2, r2, a, peer, col, part).wait_send()
        return carry

    lax.fori_loop(0, tiles, drain, 0)


def body(n_row, n_col, wavefield, recorded, v_bases, u_bases, ranks):
    tile, sources = v_bases.shape[3], wavefield.shape[2]
    both, half = v_bases.shape[2], v_bases.shape[2] // 2
    tiles, columns = u_bases.shape[0], v_bases.shape[1]
    wide = 2 * sources
    width = columns // n_row
    vmem = pl.BlockSpec(memory_space=pltpu.VMEM)
    whole = pl.BlockSpec(memory_space=pl.ANY)
    n_y = n_row // 2
    trade = pltpu.VMEM((tiles, n_col, columns, half, wide), jnp.bfloat16)
    dma = pltpu.SemaphoreType.DMA
    pair = dma((tiles, n_col, n_y))
    residual, gradient = pl.pallas_call(
        functools.partial(kernel, n_row, n_col),
        out_shape=(
            jax.ShapeDtypeStruct((tiles * tile, 2, sources), jnp.float32),
            jax.ShapeDtypeStruct((width * tile, 2, sources), jnp.float32),
        ),
        in_specs=[vmem, vmem, whole, whole, pl.BlockSpec(memory_space=pltpu.SMEM)],
        out_specs=(vmem, vmem),
        scratch_shapes=[
            pltpu.VMEM((tiles, tile, wide), jnp.float32),
            pltpu.VMEM((n_col, tiles, columns, both, tile), jnp.bfloat16),
            pltpu.VMEM((tiles, n_col, columns, both, tile), jnp.bfloat16),
            pltpu.VMEM((columns, tile, wide), jnp.bfloat16),
            trade, trade, trade, trade,
            pltpu.VMEM((columns, tile, wide), jnp.float32),
            pltpu.VMEM((n_row // 2, width, tile, wide), jnp.float32),
            pltpu.VMEM((n_row // 2, width, tile, wide), jnp.bfloat16),
            pltpu.VMEM((n_row // 2, width, tile, wide), jnp.bfloat16),
            dma((n_y,)), dma, dma((n_row,)), dma((n_row,)),
            pair, pair, pair, pair,
            dma((n_row // 2,)), dma((n_row // 2,)), dma((n_row // 2,)), dma((n_row // 2,)),
        ],
        compiler_params=pltpu.CompilerParams(
            collective_id=0, has_side_effects=True, vmem_limit_bytes=58 * 2**20
        ),
    )(
        wavefield.reshape(width, tile, wide),
        recorded,
        v_bases.reshape(n_col, tiles, columns, both, tile),
        u_bases.reshape(tiles, n_col, columns, both, tile),
        ranks.T,
    )
    return residual, gradient


def solution(mesh):
    in_specs = (
        P(("col", "row"), None, None),
        P(("row", "col"), None, None),
        P("row", "col", None, None),
        P(("row", "col"), None, None, None),
        P("row", "col"),
    )
    out_specs = (P(("row", "col"), None, None), P(("col", "row"), None, None))
    part = functools.partial(body, mesh.shape["row"], mesh.shape["col"])
    return jax.shard_map(part, mesh=mesh, in_specs=in_specs, out_specs=out_specs, check_vma=False)
```

```python
import functools

import jax
import jax.numpy as jnp
from jax import lax
from jax.experimental import pallas as pl
from jax.experimental.pallas import tpu as pltpu
from jax.sharding import PartitionSpec as P

MESH = pl.DeviceIdType.MESH


def adjoint_pair(prod, half):
    sources = prod.shape[-1] // 2
    prod = prod.reshape(-1, 2, half, 2 * sources)
    first, second = prod[:, 0], prod[:, 1]
    real = first[..., :sources] + second[..., sources:]
    imag = first[..., sources:] - second[..., :sources]
    return jnp.concatenate([real, imag], axis=-1)


def stacked(coeffs):
    sources = coeffs.shape[-1] // 2
    real, imag = coeffs[..., :sources], coeffs[..., sources:]
    second = jnp.concatenate([-imag, real], axis=-1)
    both = jnp.concatenate([coeffs, second], axis=1)
    return both.reshape(-1, 2 * sources)


def flat(bases):
    return bases.reshape(-1, bases.shape[-1])


def transposed_dot(left, right):
    return lax.dot_general(left, right, (((0,), (0,)), ((), ())), preferred_element_type=jnp.float32)


def kernel(
    n_row, n_col, wave, rec, v_hbm, u_hbm, ranks, res_out, grad_out,
    res, v, u, x, send1, recv1, send2, recv2, total, rs1, sb, rs2,
    vs, us, xs, xr, s1, r1, s2, r2, gs1, gr1, gs2, gr2,
):
    row, col = lax.axis_index("row"), lax.axis_index("col")
    y, core = row // 2, row % 2
    n_y = n_row // 2
    tiles, columns = u.shape[0], v.shape[2]
    half = v.shape[3] // 2
    tile, sources = x.shape[1], x.shape[2] // 2
    width = wave.shape[0] // tile
    group = 2 * width
    level = lax.broadcasted_iota(jnp.int32, (half, x.shape[2]), 0)

    def v_copy(part):
        span = pl.ds(part * group, group)
        return pltpu.make_async_copy(v_hbm.at[:, :, span], v.at[:, :, span], vs.at[part])

    u_copy = pltpu.make_async_copy(u_hbm, u, us)
    for k in range(n_y):
        v_copy(lax.rem(y + k, n_y)).start()
    u_copy.start()

    barrier = pltpu.get_barrier_semaphore()
    for k in range(1, n_col):
        pl.semaphore_signal(barrier, inc=1, device_id={"col": lax.rem(col + k, n_col)}, device_id_type=MESH)
    for k in range(1, n_row):
        pl.semaphore_signal(barrier, inc=1, device_id={"row": lax.rem(row + k, n_row)}, device_id_type=MESH)
    for t in range(width):
        rows = wave[pl.ds(t * tile, tile)].astype(jnp.float32)
        x[row * width + t] = jnp.concatenate([rows[:, 0], rows[:, 1]], axis=-1).astype(jnp.bfloat16)
    pl.semaphore_wait(barrier, n_col + n_row - 2)

    def wave_copy(peer, origin):
        return pltpu.make_async_remote_copy(
            src_ref=x.at[pl.ds(row * width, width)], dst_ref=x.at[pl.ds(origin * width, width)],
            send_sem=xs.at[peer], recv_sem=xr.at[origin],
            device_id={"row": peer}, device_id_type=MESH)

    def exchange(src, dst, send_sem, recv_sem, a, peer, origin, part):
        span = pl.ds(part * group, group)
        return pltpu.make_async_remote_copy(
            src_ref=src.at[a, peer, span], dst_ref=dst.at[a, origin, span],
            send_sem=send_sem.at[a, peer, part], recv_sem=recv_sem.at[a, origin, part],
            device_id={"col": peer}, device_id_type=MESH)

    wave_copy(2 * y + 1 - core, row).start()
    for k in range(1, n_y):
        for c in range(2):
            wave_copy(2 * lax.rem(y + k, n_y) + c, row).start()
    total[...] = jnp.zeros_like(total)
    for step in range(n_y):
        part = lax.rem(y + step, n_y)
        if step == 0:
            sibling = 2 * y + 1 - core
            wave_copy(sibling, sibling).wait_recv()
        else:
            for c in range(2):
                wave_copy(2 * part + c, 2 * part + c).wait_recv()
        v_copy(part).wait()

        def forward(a, carry):
            def one(t, carry):
                j = part * group + t
                prod = jnp.dot(flat(v[:, a, j]), x[j], preferred_element_type=jnp.float32)
                coeffs = adjoint_pair(prod, half)
                for d in range(n_col):
                    kept = jnp.where(level < ranks[j, d * tiles + a], coeffs[d], 0.0)
                    send1[a, d, j] = kept.astype(jnp.bfloat16)
                return carry

            lax.fori_loop(0, group, one, 0)
            for k in range(1, n_col):
                exchange(send1, recv1, s1, r1, a, lax.rem(col + k, n_col), col, part).start()
            span = pl.ds(part * group, group)
            recv1[a, col, span] = send1[a, col, span]
            return carry

        lax.fori_loop(0, tiles, forward, 0)

    u_copy.wait()
    for a in range(tiles):
        rows = rec[pl.ds(a * tile, tile)].astype(jnp.float32)
        res[a] = -jnp.concatenate([rows[:, 0], rows[:, 1]], axis=-1)

    def middle(a, carry):
        def apply(k, carry):
            origin = lax.rem(col + n_col - k, n_col)

            @pl.when(k > 0)
            def _():
                for part in range(n_y):
                    exchange(send1, recv1, s1, r1, a, origin, origin, part).wait_recv()

            res[a] += transposed_dot(flat(u[a, origin]), stacked(recv1[a, origin]))
            return carry

        lax.fori_loop(0, n_col, apply, 0)
        rounded = res[a].astype(jnp.bfloat16)

        def project(k, carry):
            peer = lax.rem(col + k, n_col)
            prod = jnp.dot(flat(u[a, peer]), rounded, preferred_element_type=jnp.float32)
            send2[a, peer] = adjoint_pair(prod, half).astype(jnp.bfloat16)

            @pl.when(k < n_col)
            def _():
                for step in range(1, n_y):
                    exchange(send2, recv2, s2, r2, a, peer, col, lax.rem(y + step, n_y)).start()

            return carry

        lax.fori_loop(1, n_col + 1, project, 0)
        for k in range(1, n_col):
            exchange(send2, recv2, s2, r2, a, lax.rem(col + k, n_col), col, y).start()
        recv2[a, col] = send2[a, col]
        for c in range(2):
            res_out[pl.ds(a * tile, tile), c] = res[a, :, c * sources:(c + 1) * sources]
        return carry

    lax.fori_loop(0, tiles, middle, 0)

    def last(a, part):
        for k in range(1, n_col):
            origin = lax.rem(col + n_col - k, n_col)
            exchange(send2, recv2, s2, r2, a, origin, origin, part).wait_recv()

        def one(t, carry):
            j = part * group + t
            kept = [
                jnp.where(level < ranks[j, s * tiles + a], recv2[a, s, j].astype(jnp.float32), 0.0).astype(jnp.bfloat16)
                for s in range(n_col)
            ]
            total[j] += transposed_dot(flat(v[:, a, j]), stacked(jnp.stack(kept)))
            return carry

        lax.fori_loop(0, group, one, 0)

    def early(a, carry):
        for step in range(1, n_y + 1):
            last(a, lax.rem(y + step, n_y))
        return carry

    lax.fori_loop(0, tiles - 1, early, 0)

    def core_copy(k):
        return pltpu.make_async_remote_copy(
            src_ref=total.at[pl.ds((2 * k + 1 - core) * width, width)], dst_ref=rs1.at[k],
            send_sem=gs1.at[k], recv_sem=gr1.at[k],
            device_id={"row": 2 * y + 1 - core}, device_id_type=MESH)

    def chip_copy(peer, origin):
        return pltpu.make_async_remote_copy(
            src_ref=sb.at[peer], dst_ref=rs2.at[origin],
            send_sem=gs2.at[peer], recv_sem=gr2.at[origin],
            device_id={"row": 2 * peer + core}, device_id_type=MESH)

    order = [lax.rem(y + k, n_y) for k in range(1, n_y)]
    for peer in order:
        last(tiles - 1, peer)
        core_copy(peer).start()
    for peer in order:
        core_copy(peer).wait_recv()
        here = total[pl.ds((2 * peer + core) * width, width)]
        sb[peer] = (here + rs1[peer]).astype(jnp.bfloat16)
        chip_copy(peer, y).start()
    last(tiles - 1, y)
    core_copy(y).start()
    core_copy(y).wait_recv()
    for peer in order:
        chip_copy(peer, peer).wait_recv()
    for t in range(width):
        grad = total[row * width + t] + rs1[y, t]
        for peer in order:
            grad += rs2[peer, t].astype(jnp.float32)
        for c in range(2):
            grad_out[pl.ds(t * tile, tile), c] = grad[:, c * sources:(c + 1) * sources]

    for k in range(1, n_row):
        wave_copy(lax.rem(row + k, n_row), row).wait_send()
    for k in range(n_y):
        core_copy(k).wait_send()
    for peer in order:
        chip_copy(peer, y).wait_send()

    def drain(a, carry):
        for k in range(1, n_col):
            peer = lax.rem(col + k, n_col)
            for part in range(n_y):
                exchange(send1, recv1, s1, r1, a, peer, col, part).wait_send()
                exchange(send2, recv2, s2, r2, a, peer, col, part).wait_send()
        return carry

    lax.fori_loop(0, tiles, drain, 0)


def body(n_row, n_col, wavefield, recorded, v_bases, u_bases, ranks):
    tile, sources = v_bases.shape[3], wavefield.shape[2]
    both, half = v_bases.shape[2], v_bases.shape[2] // 2
    tiles, columns = u_bases.shape[0], v_bases.shape[1]
    wide = 2 * sources
    width = columns // n_row
    vmem = pl.BlockSpec(memory_space=pltpu.VMEM)
    whole = pl.BlockSpec(memory_space=pl.ANY)
    n_y = n_row // 2
    trade = pltpu.VMEM((tiles, n_col, columns, half, wide), jnp.bfloat16)
    dma = pltpu.SemaphoreType.DMA
    pair = dma((tiles, n_col, n_y))
    residual, gradient = pl.pallas_call(
        functools.partial(kernel, n_row, n_col),
        out_shape=(
            jax.ShapeDtypeStruct((tiles * tile, 2, sources), jnp.float32),
            jax.ShapeDtypeStruct((width * tile, 2, sources), jnp.float32),
        ),
        in_specs=[vmem, vmem, whole, whole, pl.BlockSpec(memory_space=pltpu.SMEM)],
        out_specs=(vmem, vmem),
        scratch_shapes=[
            pltpu.VMEM((tiles, tile, wide), jnp.float32),
            pltpu.VMEM((n_col, tiles, columns, both, tile), jnp.bfloat16),
            pltpu.VMEM((tiles, n_col, columns, both, tile), jnp.bfloat16),
            pltpu.VMEM((columns, tile, wide), jnp.bfloat16),
            trade, trade, trade, trade,
            pltpu.VMEM((columns, tile, wide), jnp.float32),
            pltpu.VMEM((n_row // 2, width, tile, wide), jnp.float32),
            pltpu.VMEM((n_row // 2, width, tile, wide), jnp.bfloat16),
            pltpu.VMEM((n_row // 2, width, tile, wide), jnp.bfloat16),
            dma((n_y,)), dma, dma((n_row,)), dma((n_row,)),
            pair, pair, pair, pair,
            dma((n_row // 2,)), dma((n_row // 2,)), dma((n_row // 2,)), dma((n_row // 2,)),
        ],
        compiler_params=pltpu.CompilerParams(
            collective_id=0, has_side_effects=True, vmem_limit_bytes=58 * 2**20
        ),
    )(
        wavefield,
        recorded,
        v_bases.reshape(n_col, tiles, columns, both, tile),
        u_bases.reshape(tiles, n_col, columns, both, tile),
        ranks.T,
    )
    return residual, gradient


def solution(mesh):
    in_specs = (
        P(("col", "row"), None, None),
        P(("row", "col"), None, None),
        P("row", "col", None, None),
        P(("row", "col"), None, None, None),
        P("row", "col"),
    )
    out_specs = (P(("row", "col"), None, None), P(("col", "row"), None, None))
    part = functools.partial(body, mesh.shape["row"], mesh.shape["col"])
    return jax.shard_map(part, mesh=mesh, in_specs=in_specs, out_specs=out_specs, check_vma=False)
```
